32 devices in a mesh: blk: 4 (over z), head: 8 (over y, x, core).
Axes of the slice: x: 2, y: 2, z: 4, core: 2. Of those that a mesh axis runs over, the one named last changes fastest.
Arguments:
- latent: float32 [64, 256, 256], P('blk', 'head'), may hold values from -6 to 6
- local_gain: float32 [256], replicated, may hold values from 0.5 to 1.5
- local_project: float32 [256, 768], replicated, may hold values from -0.375 to 0.375
- local_output: float32 [256, 256], replicated, may hold values from -0.375 to 0.375
- local_scale: float32 [4], replicated, may hold values from 2 to 500
- merge_first: float32 [1024, 384], replicated, may hold values from -0.1875 to 0.1875
- merge_second: float32 [1536, 512], replicated, may hold values from -0.15625 to 0.15625
- global_gain: float32 [512], replicated, may hold values from 0.5 to 1.5
- global_project: float32 [512, 1536], replicated, may hold values from -0.25 to 0.25
- global_output: float32 [512, 512], replicated, may hold values from -0.25 to 0.25
- global_scale: float32 [8], replicated, may hold values from 2 to 500
- split_second: float32 [512, 1536], replicated, may hold values from -0.25 to 0.25
- split_first: float32 [384, 1024], replicated, may hold values from -0.3125 to 0.3125
Outputs:
- refined: float32 [64, 256, 256], P('blk', 'head')
The draws below stay inside these ranges and needn't reach their ends.
All inputs are finite; a program needn't handle non-finite values.
Results may differ from the reference program's by a relative error of at most 0.0003.
Values sent between devices are 32-bit elements; how exact they have to be, the bound alone decides.
A program may use at most 128 MiB of HBM per device.

```python
import math
import jax
import jax.numpy as jnp
from jax import lax

C0 = 256
HEAD0 = 64
CM = 384
CG = 512
HEADS_G = 8
HEAD_G = 64
HEIGHT = 64
BREADTH = 256


def scale_draw(key, how_many):
    lower, upper = (2.0, 20.0)
    exponent = jax.random.uniform(key, (how_many,), jnp.float32, math.log(lower), math.log(upper))
    return jnp.exp(exponent)


def draw_local_scale(key, part):
    return scale_draw(jax.random.fold_in(key, 11), C0 // HEAD0)


def draw_global_scale(key, part):
    return scale_draw(jax.random.fold_in(key, 23), HEADS_G)


def block_levels(rng, dims, pieces, smallest, top_value):
    def one(dim, blocks):
        steps = jax.random.uniform(jax.random.fold_in(jax.random.fold_in(rng, 6), dim), (blocks,), jnp.float32, smallest / len(pieces), top_value / len(pieces))
        return jnp.repeat(jnp.exp(steps), dims[dim] // blocks).reshape((-1,) + (1,) * (len(dims) - dim - 1))

    level = one(*pieces[0])
    for cut in pieces[1:]:
        level = level * one(*cut)
    return level


def normal_values(own_key, extent, scale, bound, shards=(), held_as=jnp.bfloat16):
    array = scale * jax.random.normal(own_key, extent, jnp.float32)
    if shards:
        array = array * block_levels(own_key, extent, shards, -0.22, 0.18)
    return jnp.clip(array, -bound, bound).astype(held_as)


def setup_inputs(seed: int = 0) -> dict:
    key_list = jax.random.split(jax.random.key(seed), 14)
    return {
        "latent": normal_values(key_list[0], (HEIGHT, BREADTH, C0), 1.0, 6.0, ((0, 4), (1, 8)), jnp.float32),
        "local_gain": jnp.clip(1.0 + 0.1 * jax.random.normal(key_list[1], (C0,), jnp.float32), 0.5, 1.5),
        "local_project": normal_values(key_list[2], (C0, 3 * C0), C0 ** -0.5, 0.375, (), jnp.float32),
        "local_output": normal_values(key_list[3], (C0, C0), C0 ** -0.5, 0.375, (), jnp.float32),
        "local_scale": draw_local_scale(jax.random.fold_in(key_list[13], 71), 0),
        "merge_first": normal_values(key_list[5], (4 * C0, CM), (4 * C0) ** -0.5, 0.1875, (), jnp.float32),
        "merge_second": normal_values(key_list[6], (4 * CM, CG), (4 * CM) ** -0.5, 0.15625, (), jnp.float32),
        "global_gain": jnp.clip(1.0 + 0.1 * jax.random.normal(key_list[7], (CG,), jnp.float32), 0.5, 1.5),
        "global_project": normal_values(key_list[8], (CG, 3 * CG), CG ** -0.5, 0.25, (), jnp.float32),
        "global_output": normal_values(key_list[9], (CG, CG), CG ** -0.5, 0.25, (), jnp.float32),
        "global_scale": draw_global_scale(jax.random.fold_in(key_list[13], 71), 0),
        "split_second": normal_values(key_list[11], (CG, 4 * CM), CG ** -0.5, 0.25, (), jnp.float32),
        "split_first": normal_values(key_list[12], (CM, 4 * C0), CM ** -0.5, 0.3125, (), jnp.float32),
    }


EPSILON = 1e-06
FLOOR_VALUE = 0.5
PRECISE = lax.Precision.HIGHEST

def matmul(left, right):
    return jnp.dot(left, right, precision=PRECISE, preferred_element_type=jnp.float32)

def rms_scale(values, gains):
    return values * lax.rsqrt(lax.optimization_barrier(jnp.mean(values * values, axis=-1, keepdims=True)) + EPSILON) * gains

def unit_rows(values):
    return values * lax.rsqrt(lax.optimization_barrier(jnp.mean(values * values, axis=-1, keepdims=True)) + EPSILON)

def floor_rows(values):
    return values * lax.rsqrt(jnp.maximum(lax.optimization_barrier(jnp.mean(values * values, axis=-1, keepdims=True)), FLOOR_VALUE))

def window_attention(queries, keys_pad, values_pad, valid, scales):
    query_rows, query_cols, head_width = (queries.shape[0], queries.shape[1], queries.shape[3])
    factor = scales / head_width
    scores = []
    for offset_row in range(7):
        for offset_col in range(7):
            nearby = keys_pad[offset_row:offset_row + query_rows, offset_col:offset_col + query_cols]
            one_score = lax.optimization_barrier(jnp.sum(queries * nearby, axis=-1)) * factor
            inside = valid[offset_row:offset_row + query_rows, offset_col:offset_col + query_cols, None] > 0
            scores.append(jnp.where(inside, one_score, -jnp.inf))
    stacked = jnp.stack(scores)
    maximum = lax.optimization_barrier(jnp.max(stacked, axis=0))
    weights = jnp.exp(stacked - maximum)
    weight_sum = lax.optimization_barrier(jnp.sum(weights, axis=0))
    mixture = jnp.zeros_like(queries)
    position = 0
    for offset_row in range(7):
        for offset_col in range(7):
            nearby = values_pad[offset_row:offset_row + query_rows, offset_col:offset_col + query_cols]
            mixture = mixture + weights[position][..., None] * nearby
            position = position + 1
    return mixture / weight_sum[..., None]

def merge_cells(grid_in):
    grid_rows, grid_cols, channels = grid_in.shape
    moved = grid_in.reshape(grid_rows // 2, 2, grid_cols // 2, 2, channels).transpose(0, 2, 1, 3, 4)
    return moved.reshape(grid_rows // 2, grid_cols // 2, 4 * channels)

def split_cells(grid_in, channels):
    grid_rows, grid_cols = (grid_in.shape[0], grid_in.shape[1])
    moved = grid_in.reshape(grid_rows, grid_cols, 2, 2, channels).transpose(0, 2, 1, 3, 4)
    return moved.reshape(2 * grid_rows, 2 * grid_cols, channels)

def global_attention(global_queries, global_keys, global_values, scales):
    token_count = global_queries.shape[0]
    block_rows = math.gcd(token_count, 1024)

    def one_head(head_items):
        head_queries, head_keys, head_values, head_scale = head_items
        factor = head_scale / head_queries.shape[1]

        def one_block(block_queries):
            scores = matmul(block_queries, head_keys.T) * factor
            maximum = lax.optimization_barrier(jnp.max(scores, axis=1, keepdims=True))
            weights = jnp.exp(scores - maximum)
            return matmul(weights, head_values) / lax.optimization_barrier(jnp.sum(weights, axis=1, keepdims=True))
        blocked = head_queries.reshape(token_count // block_rows, block_rows, head_queries.shape[1])
        return lax.map(one_block, blocked).reshape(token_count, head_queries.shape[1])
    outputs = lax.map(one_head, (jnp.transpose(global_queries, (1, 0, 2)), jnp.transpose(global_keys, (1, 0, 2)), jnp.transpose(global_values, (1, 0, 2)), scales))
    return jnp.transpose(outputs, (1, 0, 2))

def reference(latent, local_gain, local_project, local_output, local_scale, merge_first, merge_second, global_gain, global_project, global_output, global_scale, split_second, split_first):
    height, breadth = (latent.shape[0], latent.shape[1])
    heads_zero = C0 // HEAD0
    normed = rms_scale(latent, local_gain)
    projected = matmul(normed.reshape(-1, C0), local_project).reshape(height, breadth, 3, heads_zero, HEAD0)
    local_queries = unit_rows(projected[:, :, 0])
    local_keys = unit_rows(projected[:, :, 1])
    local_values = projected[:, :, 2]
    padding = ((3, 3), (3, 3), (0, 0), (0, 0))
    valid = jnp.pad(jnp.ones((height, breadth), jnp.float32), 3)
    attended = window_attention(local_queries, jnp.pad(local_keys, padding), jnp.pad(local_values, padding), valid, local_scale)
    level_zero = latent + matmul(attended.reshape(-1, C0), local_output).reshape(height, breadth, C0)
    level_one = matmul(merge_cells(level_zero).reshape(-1, 4 * C0), merge_first).reshape(height // 2, breadth // 2, CM)
    level_two = matmul(merge_cells(level_one).reshape(-1, 4 * CM), merge_second)
    normed_two = rms_scale(level_two, global_gain)
    global_proj = matmul(normed_two, global_project).reshape(-1, HEADS_G, 3, HEAD_G)
    global_queries = floor_rows(global_proj[:, :, 0])
    global_keys = floor_rows(global_proj[:, :, 1])
    global_values = global_proj[:, :, 2]
    attention_out = global_attention(global_queries, global_keys, global_values, global_scale)
    global_mixed = level_two + matmul(attention_out.reshape(-1, CG), global_output)
    up_one = split_cells(matmul(global_mixed, split_second).reshape(height // 4, breadth // 4, 4 * CM), CM) + level_one
    refined = split_cells(matmul(up_one.reshape(-1, CM), split_first).reshape(height // 2, breadth // 2, 4 * C0), C0) + level_zero
    return refined
```

```python
import functools
import math

import jax
import jax.numpy as jnp
from jax import lax
from jax.experimental import pallas as pl
from jax.experimental.pallas import tpu as pltpu
from jax.sharding import PartitionSpec as P

C0 = 256
HEAD0 = 64
CM = 384
HEADS_G = 8
HEAD_G = 64


EPSILON = 1e-06
FLOOR_VALUE = 0.5
PRECISE = lax.Precision.HIGHEST


def matmul(left, right):
    return jnp.dot(left, right, precision=PRECISE, preferred_element_type=jnp.float32)


def rms_scale(values, gains):
    return values * lax.rsqrt(jnp.mean(values * values, axis=-1, keepdims=True) + EPSILON) * gains


def unit_rows(values):
    return values * lax.rsqrt(jnp.mean(values * values, axis=-1, keepdims=True) + EPSILON)


def floor_rows(values):
    return values * lax.rsqrt(
        jnp.maximum(jnp.mean(values * values, axis=-1, keepdims=True), FLOOR_VALUE)
    )


def split_cells(grid_in, channels):
    grid_rows, grid_cols = (grid_in.shape[0], grid_in.shape[1])
    moved = grid_in.reshape(grid_rows, grid_cols, 2, 2, channels).transpose(0, 2, 1, 3, 4)
    return moved.reshape(2 * grid_rows, 2 * grid_cols, channels)


MESH = pl.DeviceIdType.MESH
HALO = 3
EDGE = 8
LANES = 128
LOG2E = math.log2(math.e)
DIRECTIONS = ((-1, 0), (1, 0), (0, -1), (0, 1), (-1, -1), (-1, 1), (1, -1), (1, 1))


def halves(values):
    high = values.astype(jnp.bfloat16)
    return high, (values - high.astype(jnp.float32)).astype(jnp.bfloat16)


def plain_dot(left, right):
    return jnp.dot(left, right, preferred_element_type=jnp.float32)


def split_dot(left, right):
    left_high, left_low = halves(left)
    right_high, right_low = halves(right)
    return (
        plain_dot(left_low, right_high)
        + plain_dot(left_high, right_low)
        + plain_dot(left_high, right_high)
    )


def group_matrix(width, group):
    rows = lax.broadcasted_iota(jnp.int32, (width, width), 0) // group
    cols = lax.broadcasted_iota(jnp.int32, (width, width), 1) // group
    return jnp.where(rows == cols, 1.0 / group, 0.0).astype(jnp.bfloat16)


def group_mean_squares(values, group):
    high, low = halves(values * values)
    matrix = group_matrix(values.shape[1], group)
    return plain_dot(high, matrix) + plain_dot(low, matrix)


def neighbours(sizes):
    blk, head = lax.axis_index("blk"), lax.axis_index("head")
    for dz, dc in DIRECTIONS:
        row, col = blk + dz, head + dc
        back_row, back_col = blk - dz, head - dc
        there = (row >= 0) & (row < sizes[0]) & (col >= 0) & (col < sizes[1])
        back = (back_row >= 0) & (back_row < sizes[0]) & (back_col >= 0) & (back_col < sizes[1])
        yield (row, col), there, back


def local_kernel(
    sizes,
    latent_ref,
    gain_ref,
    project_ref,
    output_ref,
    scale_ref,
    merge_first_ref,
    merge_second_ref,
    global_gain_ref,
    zero_ref,
    one_ref,
    two_ref,
    normed_ref,
    up_ref,
    down_ref,
    left_ref,
    right_ref,
    query_ref,
    key_ref,
    high_ref,
    low_ref,
    attended_ref,
    zero_chunks,
    one_chunks,
    send_sem,
    recv_sem,
):
    rows, cols, width = latent_ref.shape
    heads = width // HEAD0
    span = cols + EDGE
    low_row, low_col = rows - HALO, cols - EDGE
    blk, head = lax.axis_index("blk"), lax.axis_index("head")
    barrier = pltpu.get_barrier_semaphore()
    count = jnp.int32(0)
    for device, there, back in neighbours(sizes):
        count = count + there.astype(jnp.int32)

        @pl.when(there)
        def _(device=device):
            pl.semaphore_signal(barrier, inc=1, device_id=device, device_id_type=MESH)

    pl.semaphore_wait(barrier, count)

    sources = {-1: slice(0, HALO), 1: slice(low_row, rows)}
    corner_rows = {-1: slice(rows + HALO, rows + 2 * HALO), 1: slice(0, HALO)}
    columns = {-1: slice(0, EDGE), 1: slice(low_col, cols)}

    def copy_of(index, device):
        dz, dc = DIRECTIONS[index]
        if dc == 0:
            source = latent_ref.at[sources[dz]]
            target = down_ref if dz < 0 else up_ref
        else:
            side = right_ref if dc < 0 else left_ref
            if dz == 0:
                source = latent_ref.at[:, columns[dc]]
                target = side.at[HALO : HALO + rows]
            else:
                source = latent_ref.at[sources[dz], columns[dc]]
                target = side.at[corner_rows[dz]]
        return pltpu.make_async_remote_copy(
            src_ref=source,
            dst_ref=target,
            send_sem=send_sem.at[index],
            recv_sem=recv_sem.at[index],
            device_id=device,
            device_id_type=MESH,
        )

    for index, (device, there, back) in enumerate(neighbours(sizes)):

        @pl.when(there)
        def _(index=index, device=device):
            copy_of(index, device).start()

    gain = gain_ref[...]
    head_factor = jnp.concatenate(
        [jnp.full((1, HEAD0), scale_ref[0, h] * (LOG2E / HEAD0), jnp.float32) for h in range(heads)],
        axis=1,
    )
    latent = latent_ref[...].reshape(rows * cols, width)
    normed = rms_scale(latent, gain)
    queries = split_dot(normed, project_ref[:, :width])
    queries = queries * lax.rsqrt(group_mean_squares(queries, HEAD0) + EPSILON) * head_factor
    high, low = halves(queries)
    for h in range(heads):
        a, b = high[:, h * HEAD0 : (h + 1) * HEAD0], low[:, h * HEAD0 : (h + 1) * HEAD0]
        query_ref[h] = jnp.concatenate([a, a, b, b], axis=1)

    for index, (device, there, back) in enumerate(neighbours(sizes)):

        @pl.when(back)
        def _(index=index, device=device):
            copy_of(index, device).wait_recv()

        @pl.when(there)
        def _(index=index, device=device):
            copy_of(index, device).wait_send()

    has_up, has_down = blk > 0, blk < sizes[0] - 1
    has_left, has_right = head > 0, head < sizes[1] - 1
    middle = jnp.concatenate(
        [
            jnp.where(has_up, up_ref[...], 0.0),
            latent_ref[...],
            jnp.where(has_down, down_ref[...], 0.0),
        ],
        axis=0,
    )
    shape = (rows + 2 * HALO, EDGE, width)
    spot = lax.broadcasted_iota(jnp.int32, shape, 1)
    layer = lax.broadcasted_iota(jnp.int32, shape, 0)
    row_there = (has_up | (layer >= HALO)) & (has_down | (layer < rows + HALO))
    side = jnp.where(
        (spot < HALO) & has_right & row_there,
        right_ref[...],
        jnp.where((spot >= EDGE - HALO) & has_left & row_there, left_ref[...], 0.0),
    )
    padded_rows = rows + 2 * HALO
    total = padded_rows * span
    everything = jnp.concatenate([middle, side], axis=1).reshape(total, width)
    keyvals = split_dot(rms_scale(everything, gain), project_ref[:, width:])
    keys = keyvals[:, :width]
    keys = keys * lax.rsqrt(group_mean_squares(keys, HEAD0) + EPSILON)
    high, low = halves(keys)
    value_high, value_low = halves(keyvals[:, width:])
    for h in range(heads):
        part = slice(h * HEAD0, (h + 1) * HEAD0)
        a, b = high[:, part], low[:, part]
        key_ref[h] = jnp.concatenate([a, b, a, b], axis=1)
        high_ref[h] = jnp.concatenate([value_high[:, part], value_low[:, part]], axis=1)
        low_ref[h] = value_high[:, part]

    step_rows = 4
    block = step_rows * cols
    reach = (step_rows + 2 * HALO) * span
    query_at = lax.broadcasted_iota(jnp.int32, (block, 1), 0)
    key_at = lax.broadcasted_iota(jnp.int32, (1, reach), 1)
    query_row, query_col = query_at // cols, query_at % cols
    key_row, place = key_at // span, key_at % span
    key_col = jnp.where(
        place < cols + HALO,
        place,
        jnp.where(place >= span - HALO, place - span, -4 * span),
    )
    col_here = (
        (key_col + head * cols >= 0)
        & (key_col + head * cols < sizes[1] * cols)
    )
    key_col = jnp.where(col_here, key_col, -4 * span)
    row_gap, col_gap = key_row - query_row, key_col - query_col
    near = (row_gap >= 0) & (row_gap <= 2 * HALO) & (col_gap >= -HALO) & (col_gap <= HALO)
    near_bias = jnp.where(near, 0.0, -1e30)

    def attend(step, unused):
        grid_row = blk * rows + step * step_rows - HALO + key_row
        bias = near_bias + jnp.where(
            (grid_row >= 0) & (grid_row < sizes[0] * rows), 0.0, -1e30
        )
        queries_at = pl.ds(pl.multiple_of(step * block, block), block)
        keys_at = pl.ds(pl.multiple_of(step * step_rows * span, step_rows * span), reach)
        parts = []
        for h in range(heads):
            scores = (
                lax.dot_general(
                    query_ref[h, queries_at],
                    key_ref[h, keys_at],
                    (((1,), (1,)), ((), ())),
                    preferred_element_type=jnp.float32,
                )
                + bias
            )
            weights = jnp.exp2(scores - jnp.max(scores, axis=1, keepdims=True))
            weight_sum = jnp.sum(weights, axis=1, keepdims=True)
            weight_high, weight_low = halves(weights)
            wide = plain_dot(weight_high, high_ref[h, keys_at])
            mixture = (
                wide[:, :HEAD0]
                + wide[:, HEAD0:]
                + plain_dot(weight_low, low_ref[h, keys_at])
            )
            parts.append(mixture / weight_sum)
        attended_ref[queries_at] = jnp.concatenate(parts, axis=1)
        return unused

    lax.fori_loop(0, rows // step_rows, attend, 0)
    zero = latent + split_dot(attended_ref[...], output_ref[...])
    zero_ref[...] = zero
    store_chunks(zero_chunks, zero)
    merged = merge_from(zero_chunks, rows, cols)
    one = split_dot(merged, merge_first_ref[...])
    one_ref[...] = one
    store_chunks(one_chunks, one)
    merged = merge_from(one_chunks, rows // 2, cols // 2)
    two = split_dot(merged, merge_second_ref[...])
    two_ref[...] = two
    normed_ref[...] = rms_scale(two, global_gain_ref[...])


def store_chunks(ref, values):
    for chunk in range(ref.shape[0]):
        ref[chunk] = values[:, chunk * LANES : (chunk + 1) * LANES]


def merge_from(ref, rows, cols):
    cells, width = rows * cols, ref.shape[0] * LANES
    evens, odds = (
        jnp.concatenate(
            [
                ref[chunk, pl.ds(start, cells // 2, stride=2)]
                for chunk in range(ref.shape[0])
            ],
            axis=1,
        ).reshape(rows // 2, 2, cols // 2, width)
        for start in (0, 1)
    )
    pieces = [
        source[:, which].reshape(cells // 4, width)
        for which in (0, 1)
        for source in (evens, odds)
    ]
    return jnp.concatenate(pieces, axis=1)


def local_part(latent, gain, project, output, scale, merge_first, merge_second, global_gain):
    rows, cols, width = latent.shape
    sizes = (lax.axis_size("blk"), lax.axis_size("head"))
    heads = width // HEAD0
    total = (rows + 2 * HALO) * (cols + EDGE)
    vmem = pl.BlockSpec(memory_space=pltpu.VMEM)
    mid, coarse = merge_first.shape[1], merge_second.shape[1]
    f32, b16 = jnp.float32, jnp.bfloat16
    return pl.pallas_call(
        functools.partial(local_kernel, sizes),
        out_shape=[
            jax.ShapeDtypeStruct((rows * cols, width), f32),
            jax.ShapeDtypeStruct((rows * cols // 4, mid), f32),
            jax.ShapeDtypeStruct((rows * cols // 16, coarse), f32),
            jax.ShapeDtypeStruct((rows * cols // 16, coarse), f32),
        ],
        in_specs=[vmem] * 4 + [pl.BlockSpec(memory_space=pltpu.SMEM)] + [vmem] * 3,
        out_specs=[vmem] * 4,
        scratch_shapes=[
            pltpu.VMEM((HALO, cols, width), f32),
            pltpu.VMEM((HALO, cols, width), f32),
            pltpu.VMEM((rows + 2 * HALO, EDGE, width), f32),
            pltpu.VMEM((rows + 2 * HALO, EDGE, width), f32),
            pltpu.VMEM((heads, rows * cols, 4 * HEAD0), b16),
            pltpu.VMEM((heads, total, 4 * HEAD0), b16),
            pltpu.VMEM((heads, total, 2 * HEAD0), b16),
            pltpu.VMEM((heads, total, HEAD0), b16),
            pltpu.VMEM((rows * cols, width), f32),
            pltpu.VMEM((width // LANES, rows * cols, LANES), f32),
            pltpu.VMEM((mid // LANES, rows * cols // 4, LANES), f32),
            pltpu.SemaphoreType.DMA((8,)),
            pltpu.SemaphoreType.DMA((8,)),
        ],
        compiler_params=pltpu.CompilerParams(
            collective_id=0, has_side_effects=True, vmem_limit_bytes=48 * 2**20
        ),
        name="local_part",
    )(
        latent,
        gain[None],
        project,
        output,
        scale[None],
        merge_first,
        merge_second,
        global_gain[None],
    )


def shards(
    latent,
    local_gain,
    local_project,
    local_output,
    local_scale,
    merge_first,
    merge_second,
    global_gain,
    global_project,
    global_output,
    global_scale,
    split_second,
    split_first,
):
    tile_rows, tile_cols = (latent.shape[0], latent.shape[1])
    level_zero, level_one, level_two, normed_two = local_part(
        latent,
        local_gain,
        local_project,
        local_output,
        local_scale,
        merge_first,
        merge_second,
        global_gain,
    )
    level_zero = level_zero.reshape(tile_rows, tile_cols, C0)
    level_one = level_one.reshape(tile_rows // 2, tile_cols // 2, CM)
    own_tokens = level_two.shape[0]
    group_size = lax.axis_size("head")
    copies = group_size // HEADS_G
    position = lax.axis_index("head")
    head_id = position // copies
    part_id = position % copies
    span = HEADS_G * own_tokens
    own_project = lax.dynamic_slice_in_dim(global_project, head_id * 3 * HEAD_G, 3 * HEAD_G, 1)
    projected = matmul(lax.all_gather(normed_two, "head", axis=0, tiled=True), own_project)
    projected = projected.reshape(-1, 1, 3, HEAD_G)
    query_part = lax.dynamic_slice_in_dim(projected[:, :, 0], part_id * span, span, 0)
    global_queries = floor_rows(query_part)
    global_keys = floor_rows(projected[:, :, 1])
    global_values = projected[:, :, 2]
    own_scale = lax.dynamic_slice_in_dim(global_scale, head_id, 1, 0)
    factor = own_scale / HEAD_G
    query_count = global_queries.shape[0]
    starting = (
        jnp.full((1, query_count), -jnp.inf, jnp.float32),
        jnp.zeros((1, query_count), jnp.float32),
        jnp.zeros((1, query_count, HEAD_G), jnp.float32),
    )
    running = starting
    key_piece = lax.all_gather(global_keys, "blk", axis=0, tiled=True)
    value_piece = lax.all_gather(global_values, "blk", axis=0, tiled=True)
    piece_rows = key_piece.shape[0]
    block_rows = math.gcd(piece_rows, 2048)
    key_blocks = key_piece.reshape(piece_rows // block_rows, block_rows, 1, HEAD_G)
    value_blocks = value_piece.reshape(piece_rows // block_rows, block_rows, 1, HEAD_G)

    def advance(current, blocks_now):
        key_block, value_block = blocks_now
        best_score, weight_sum, accumulated = current
        scores = (
            jnp.einsum(
                "qhd,khd->hqk",
                global_queries,
                key_block,
                precision=PRECISE,
                preferred_element_type=jnp.float32,
            )
            * factor[:, None, None]
        )
        raised_best = jnp.maximum(best_score, jnp.max(scores, axis=2))
        rescale = jnp.exp(best_score - raised_best)
        weights = jnp.exp(scores - raised_best[:, :, None])
        weight_sum = weight_sum * rescale + jnp.sum(weights, axis=2)
        accumulated = accumulated * rescale[:, :, None] + jnp.einsum(
            "hqk,khd->hqd",
            weights,
            value_block,
            precision=PRECISE,
            preferred_element_type=jnp.float32,
        )
        return ((raised_best, weight_sum, accumulated), None)

    running, unused = lax.scan(advance, running, (key_blocks, value_blocks))
    best_score, weight_sum, accumulated = running
    attention_out = (accumulated / weight_sum[:, :, None])[0]
    placed = lax.dynamic_update_slice_in_dim(
        jnp.zeros((group_size * own_tokens, HEAD_G), jnp.float32), attention_out, part_id * span, 0
    )
    own_output = lax.dynamic_slice_in_dim(global_output, head_id * HEAD_G, HEAD_G, 0)
    mixed_global = lax.psum_scatter(
        matmul(placed, own_output), "head", scatter_dimension=0, tiled=True
    )
    global_mixed = level_two + mixed_global
    up_one = (
        split_cells(
            matmul(global_mixed, split_second).reshape(tile_rows // 4, tile_cols // 4, 4 * CM), CM
        )
        + level_one
    )
    refined = (
        split_cells(
            matmul(up_one.reshape(-1, CM), split_first).reshape(
                tile_rows // 2, tile_cols // 2, 4 * C0
            ),
            C0,
        )
        + level_zero
    )
    return refined


def solution(mesh):
    in_specs = (P("blk", "head", None), P(), P(), P(), P(), P(), P(), P(), P(), P(), P(), P(), P())
    out_specs = P("blk", "head", None)
    return jax.shard_map(shards, mesh=mesh, in_specs=in_specs, out_specs=out_specs, check_vma=False)
```

```python
import functools
import math

import jax
import jax.numpy as jnp
from jax import lax
from jax.experimental import pallas as pl
from jax.experimental.pallas import tpu as pltpu
from jax.sharding import PartitionSpec as P

C0 = 256
HEAD0 = 64
HEADS_G = 8
HEAD_G = 64


EPSILON = 1e-06
FLOOR_VALUE = 0.5


def rms_scale(values, gains):
    return values * lax.rsqrt(jnp.mean(values * values, axis=-1, keepdims=True) + EPSILON) * gains


def floor_rows(values):
    return values * lax.rsqrt(
        jnp.maximum(jnp.mean(values * values, axis=-1, keepdims=True), FLOOR_VALUE)
    )


MESH = pl.DeviceIdType.MESH
HALO = 3
EDGE = 8
LANES = 128
LOG2E = math.log2(math.e)
DIRECTIONS = ((-1, 0), (1, 0), (0, -1), (0, 1), (-1, -1), (-1, 1), (1, -1), (1, 1))


def halves(values):
    high = values.astype(jnp.bfloat16)
    return high, (values - high.astype(jnp.float32)).astype(jnp.bfloat16)


def plain_dot(left, right):
    return jnp.dot(left, right, preferred_element_type=jnp.float32)


def split_dot(left, right):
    left_high, left_low = halves(left)
    right_high, right_low = halves(right)
    return (
        plain_dot(left_low, right_high)
        + plain_dot(left_high, right_low)
        + plain_dot(left_high, right_high)
    )


def group_matrix(width, group):
    rows = lax.broadcasted_iota(jnp.int32, (width, width), 0) // group
    cols = lax.broadcasted_iota(jnp.int32, (width, width), 1) // group
    return jnp.where(rows == cols, 1.0 / group, 0.0).astype(jnp.bfloat16)


def group_mean_squares(values, group):
    high, low = halves(values * values)
    matrix = group_matrix(values.shape[1], group)
    return plain_dot(high, matrix) + plain_dot(low, matrix)


def neighbours(sizes):
    blk, head = lax.axis_index("blk"), lax.axis_index("head")
    for dz, dc in DIRECTIONS:
        row, col = blk + dz, head + dc
        back_row, back_col = blk - dz, head - dc
        there = (row >= 0) & (row < sizes[0]) & (col >= 0) & (col < sizes[1])
        back = (back_row >= 0) & (back_row < sizes[0]) & (back_col >= 0) & (back_col < sizes[1])
        yield (row, col), there, back


def local_kernel(
    sizes,
    latent_ref,
    gain_ref,
    project_ref,
    output_hbm,
    scale_ref,
    merge_first_hbm,
    merge_second_hbm,
    global_gain_ref,
    zero_ref,
    one_ref,
    two_ref,
    normed_ref,
    up_ref,
    down_ref,
    left_ref,
    right_ref,
    query_ref,
    key_ref,
    high_ref,
    low_ref,
    attended_ref,
    zero_chunks,
    one_chunks,
    output_ref,
    merge_first_ref,
    merge_second_ref,
    weight_sem,
    send_sem,
    recv_sem,
):
    rows, cols, width = latent_ref.shape
    heads = width // HEAD0
    span = cols + EDGE
    low_row, low_col = rows - HALO, cols - EDGE
    blk, head = lax.axis_index("blk"), lax.axis_index("head")
    barrier = pltpu.get_barrier_semaphore()
    count = jnp.int32(0)
    for device, there, back in neighbours(sizes):
        count = count + there.astype(jnp.int32)

        @pl.when(there)
        def _(device=device):
            pl.semaphore_signal(barrier, inc=1, device_id=device, device_id_type=MESH)

    fetches = [
        pltpu.make_async_copy(source, target, weight_sem.at[index])
        for index, (source, target) in enumerate(
            (
                (output_hbm, output_ref),
                (merge_first_hbm, merge_first_ref),
                (merge_second_hbm, merge_second_ref),
            )
        )
    ]
    for fetch in fetches:
        fetch.start()
    pl.semaphore_wait(barrier, count)

    sources = {-1: slice(0, HALO), 1: slice(low_row, rows)}
    corner_rows = {-1: slice(rows + HALO, rows + 2 * HALO), 1: slice(0, HALO)}
    columns = {-1: slice(0, EDGE), 1: slice(low_col, cols)}

    def copy_of(index, device):
        dz, dc = DIRECTIONS[index]
        if dc == 0:
            source = latent_ref.at[sources[dz]]
            target = down_ref if dz < 0 else up_ref
        else:
            side = right_ref if dc < 0 else left_ref
            if dz == 0:
                source = latent_ref.at[:, columns[dc]]
                target = side.at[HALO : HALO + rows]
            else:
                source = latent_ref.at[sources[dz], columns[dc]]
                target = side.at[corner_rows[dz]]
        return pltpu.make_async_remote_copy(
            src_ref=source,
            dst_ref=target,
            send_sem=send_sem.at[index],
            recv_sem=recv_sem.at[index],
            device_id=device,
            device_id_type=MESH,
        )

    for index, (device, there, back) in enumerate(neighbours(sizes)):

        @pl.when(there)
        def _(index=index, device=device):
            copy_of(index, device).start()

    gain = gain_ref[...]
    head_factor = jnp.concatenate(
        [jnp.full((1, HEAD0), scale_ref[0, h] * (LOG2E / HEAD0), jnp.float32) for h in range(heads)],
        axis=1,
    )
    latent = latent_ref[...].reshape(rows * cols, width)
    normed = rms_scale(latent, gain)
    queries = split_dot(normed, project_ref[:, :width])
    queries = queries * lax.rsqrt(group_mean_squares(queries, HEAD0) + EPSILON) * head_factor
    high, low = halves(queries)
    for h in range(heads):
        a, b = high[:, h * HEAD0 : (h + 1) * HEAD0], low[:, h * HEAD0 : (h + 1) * HEAD0]
        query_ref[h] = jnp.concatenate([a, a, b, b], axis=1)

    for index, (device, there, back) in enumerate(neighbours(sizes)):

        @pl.when(back)
        def _(index=index, device=device):
            copy_of(index, device).wait_recv()

        @pl.when(there)
        def _(index=index, device=device):
            copy_of(index, device).wait_send()

    has_up, has_down = blk > 0, blk < sizes[0] - 1
    has_left, has_right = head > 0, head < sizes[1] - 1
    middle = jnp.concatenate(
        [
            jnp.where(has_up, up_ref[...], 0.0),
            latent_ref[...],
            jnp.where(has_down, down_ref[...], 0.0),
        ],
        axis=0,
    )
    shape = (rows + 2 * HALO, EDGE, width)
    spot = lax.broadcasted_iota(jnp.int32, shape, 1)
    layer = lax.broadcasted_iota(jnp.int32, shape, 0)
    row_there = (has_up | (layer >= HALO)) & (has_down | (layer < rows + HALO))
    side = jnp.where(
        (spot < HALO) & has_right & row_there,
        right_ref[...],
        jnp.where((spot >= EDGE - HALO) & has_left & row_there, left_ref[...], 0.0),
    )
    padded_rows = rows + 2 * HALO
    total = padded_rows * span
    everything = jnp.concatenate([middle, side], axis=1).reshape(total, width)
    keyvals = split_dot(rms_scale(everything, gain), project_ref[:, width:])
    keys = keyvals[:, :width]
    keys = keys * lax.rsqrt(group_mean_squares(keys, HEAD0) + EPSILON)
    high, low = halves(keys)
    value_high, value_low = halves(keyvals[:, width:])
    for h in range(heads):
        part = slice(h * HEAD0, (h + 1) * HEAD0)
        a, b = high[:, part], low[:, part]
        key_ref[h] = jnp.concatenate([a, b, a, b], axis=1)
        high_ref[h] = jnp.concatenate([value_high[:, part], value_low[:, part]], axis=1)
        low_ref[h] = value_high[:, part]

    step_rows = 4
    block = step_rows * cols
    reach = (step_rows + 2 * HALO) * span
    query_at = lax.broadcasted_iota(jnp.int32, (block, 1), 0)
    key_at = lax.broadcasted_iota(jnp.int32, (1, reach), 1)
    query_row, query_col = query_at // cols, query_at % cols
    key_row, place = key_at // span, key_at % span
    key_col = jnp.where(
        place < cols + HALO,
        place,
        jnp.where(place >= span - HALO, place - span, -4 * span),
    )
    col_here = (
        (key_col + head * cols >= 0)
        & (key_col + head * cols < sizes[1] * cols)
    )
    key_col = jnp.where(col_here, key_col, -4 * span)
    row_gap, col_gap = key_row - query_row, key_col - query_col
    near = (row_gap >= 0) & (row_gap <= 2 * HALO) & (col_gap >= -HALO) & (col_gap <= HALO)
    near_bias = jnp.where(near, 0.0, -1e30)

    def attend(step, unused):
        grid_row = blk * rows + step * step_rows - HALO + key_row
        bias = near_bias + jnp.where(
            (grid_row >= 0) & (grid_row < sizes[0] * rows), 0.0, -1e30
        )
        queries_at = pl.ds(pl.multiple_of(step * block, block), block)
        keys_at = pl.ds(pl.multiple_of(step * step_rows * span, step_rows * span), reach)
        parts = []
        for h in range(heads):
            scores = (
                lax.dot_general(
                    query_ref[h, queries_at],
                    key_ref[h, keys_at],
                    (((1,), (1,)), ((), ())),
                    preferred_element_type=jnp.float32,
                )
                + bias
            )
            weights = jnp.exp2(scores - jnp.max(scores, axis=1, keepdims=True))
            weight_sum = jnp.sum(weights, axis=1, keepdims=True)
            weight_high, weight_low = halves(weights)
            wide = plain_dot(weight_high, high_ref[h, keys_at])
            mixture = (
                wide[:, :HEAD0]
                + wide[:, HEAD0:]
                + plain_dot(weight_low, low_ref[h, keys_at])
            )
            parts.append(mixture / weight_sum)
        attended_ref[queries_at] = jnp.concatenate(parts, axis=1)
        return unused

    lax.fori_loop(0, rows // step_rows, attend, 0)
    for fetch in fetches:
        fetch.wait()
    zero = latent + split_dot(attended_ref[...], output_ref[...])
    zero_ref[...] = zero
    store_chunks(zero_chunks, zero)
    merged = merge_from(zero_chunks, rows, cols)
    one = split_dot(merged, merge_first_ref[...])
    store_chunks(one_chunks, one)
    merged = merge_from(one_chunks, rows // 2, cols // 2)
    one_ref[...] = merged
    two = split_dot(merged, merge_second_ref[...])
    two_ref[...] = two
    normed_ref[...] = rms_scale(two, global_gain_ref[...])


def store_chunks(ref, values):
    for chunk in range(ref.shape[0]):
        ref[chunk] = values[:, chunk * LANES : (chunk + 1) * LANES]


def merge_from(ref, rows, cols):
    cells, width = rows * cols, ref.shape[0] * LANES
    evens, odds = (
        jnp.concatenate(
            [
                ref[chunk, pl.ds(start, cells // 2, stride=2)]
                for chunk in range(ref.shape[0])
            ],
            axis=1,
        ).reshape(rows // 2, 2, cols // 2, width)
        for start in (0, 1)
    )
    pieces = [
        source[:, which].reshape(cells // 4, width)
        for which in (0, 1)
        for source in (evens, odds)
    ]
    return jnp.concatenate(pieces, axis=1)


def local_part(latent, gain, project, output, scale, merge_first, merge_second, global_gain):
    rows, cols, width = latent.shape
    sizes = (lax.axis_size("blk"), lax.axis_size("head"))
    heads = width // HEAD0
    total = (rows + 2 * HALO) * (cols + EDGE)
    vmem = pl.BlockSpec(memory_space=pltpu.VMEM)
    hbm = pl.BlockSpec(memory_space=pl.ANY)
    mid, coarse = merge_first.shape[1], merge_second.shape[1]
    f32, b16 = jnp.float32, jnp.bfloat16
    return pl.pallas_call(
        functools.partial(local_kernel, sizes),
        out_shape=[
            jax.ShapeDtypeStruct((rows * cols, width), f32),
            jax.ShapeDtypeStruct((rows * cols // 16, 4 * mid), f32),
            jax.ShapeDtypeStruct((rows * cols // 16, coarse), f32),
            jax.ShapeDtypeStruct((rows * cols // 16, coarse), f32),
        ],
        in_specs=[vmem] * 3 + [hbm, pl.BlockSpec(memory_space=pltpu.SMEM), hbm, hbm, vmem],
        out_specs=[vmem] * 4,
        scratch_shapes=[
            pltpu.VMEM((HALO, cols, width), f32),
            pltpu.VMEM((HALO, cols, width), f32),
            pltpu.VMEM((rows + 2 * HALO, EDGE, width), f32),
            pltpu.VMEM((rows + 2 * HALO, EDGE, width), f32),
            pltpu.VMEM((heads, rows * cols, 4 * HEAD0), b16),
            pltpu.VMEM((heads, total, 4 * HEAD0), b16),
            pltpu.VMEM((heads, total, 2 * HEAD0), b16),
            pltpu.VMEM((heads, total, HEAD0), b16),
            pltpu.VMEM((rows * cols, width), f32),
            pltpu.VMEM((width // LANES, rows * cols, LANES), f32),
            pltpu.VMEM((mid // LANES, rows * cols // 4, LANES), f32),
            pltpu.VMEM(output.shape, f32),
            pltpu.VMEM(merge_first.shape, f32),
            pltpu.VMEM(merge_second.shape, f32),
            pltpu.SemaphoreType.DMA((3,)),
            pltpu.SemaphoreType.DMA((8,)),
            pltpu.SemaphoreType.DMA((8,)),
        ],
        compiler_params=pltpu.CompilerParams(
            collective_id=0, has_side_effects=True, vmem_limit_bytes=48 * 2**20
        ),
        name="local_part",
    )(
        latent,
        gain[None],
        project,
        output,
        scale[None],
        merge_first,
        merge_second,
        global_gain[None],
    )


def global_kernel(
    sizes,
    normed_ref,
    two_ref,
    one_ref,
    zero_ref,
    scale_ref,
    project_hbm,
    output_hbm,
    split_second_hbm,
    split_first_hbm,
    refined_ref,
    gather_ref,
    proj_ref,
    outgoing_ref,
    incoming_ref,
    result_ref,
    attended_ref,
    spread_ref,
    project_ref,
    output_ref,
    split_second_ref,
    split_first_ref,
    weight_sem,
    send_one,
    recv_one,
    send_two,
    recv_two,
    send_three,
    recv_three,
    grid,
):
    blocks, group = sizes
    rows, cols = grid
    tokens, width = normed_ref.shape
    copies = group // HEADS_G
    blk, me = lax.axis_index("blk"), lax.axis_index("head")
    column = [((blk + d) % blocks, (blk + blocks - d) % blocks) for d in range(1, blocks)]
    line = [((me + d) % group, (me + group - d) % group) for d in range(1, group)]

    fetches = [
        pltpu.make_async_copy(source, target, weight_sem.at[index])
        for index, (source, target) in enumerate(
            (
                (project_hbm, project_ref),
                (output_hbm, output_ref),
                (split_second_hbm, split_second_ref),
                (split_first_hbm, split_first_ref),
            )
        )
    ]
    barrier = pltpu.get_barrier_semaphore()
    for peer, unused in column:
        pl.semaphore_signal(barrier, inc=1, device_id=(peer, me), device_id_type=MESH)
    for peer, unused in line:
        pl.semaphore_signal(barrier, inc=1, device_id=(blk, peer), device_id_type=MESH)
    for fetch in fetches:
        fetch.start()
    pl.semaphore_wait(barrier, blocks + group - 2)

    first = [
        pltpu.make_async_remote_copy(
            src_ref=normed_ref,
            dst_ref=gather_ref.at[blk],
            send_sem=send_one.at[index],
            recv_sem=recv_one.at[index],
            device_id=(peer, me),
            device_id_type=MESH,
        )
        for index, (peer, unused) in enumerate(column)
    ]
    for copy in first:
        copy.start()
    gather_ref[blk] = normed_ref[...]
    fetches[0].wait()
    for copy in first:
        copy.wait_recv()
    gathered = gather_ref[...].reshape(blocks * tokens, width)
    projected = split_dot(gathered, project_ref[...])
    proj_ref[...] = projected.reshape(blocks, tokens, projected.shape[1])
    own = proj_ref[blk]
    blank = jnp.zeros((tokens, HEAD_G), jnp.float32)
    for h in range(HEADS_G):
        start = 3 * HEAD_G * h
        keys = floor_rows(projected[:, start + HEAD_G : start + 2 * HEAD_G])
        values = projected[:, start + 2 * HEAD_G : start + 3 * HEAD_G]
        queries = floor_rows(own[:, start : start + HEAD_G])
        outgoing_ref[h, : blocks * tokens] = jnp.concatenate([keys, values], axis=1)
        outgoing_ref[h, blocks * tokens :] = jnp.concatenate([queries, blank], axis=1)

    second = [
        pltpu.make_async_remote_copy(
            src_ref=outgoing_ref.at[peer // copies],
            dst_ref=incoming_ref.at[me],
            send_sem=send_two.at[index],
            recv_sem=recv_two.at[index],
            device_id=(blk, peer),
            device_id_type=MESH,
        )
        for index, (peer, unused) in enumerate(line)
    ]
    for copy in second:
        copy.start()
    incoming_ref[me] = outgoing_ref[me // copies]
    for copy in second:
        copy.wait_recv()

    factor = scale_ref[0, me // copies] * (LOG2E / HEAD_G)
    part = me % copies
    queries = incoming_ref[pl.ds(part * HEADS_G, HEADS_G), blocks * tokens :, :HEAD_G]
    high, low = halves(queries.reshape(HEADS_G * tokens, HEAD_G) * factor)
    query_cat = jnp.concatenate([high, high, low, low], axis=1)
    keyvals = incoming_ref[:, : blocks * tokens].reshape(group * blocks * tokens, 2 * HEAD_G)
    high, low = halves(keyvals)
    key_high, key_low = high[:, :HEAD_G], low[:, :HEAD_G]
    value_high, value_low = high[:, HEAD_G:], low[:, HEAD_G:]
    key_cat = jnp.concatenate([key_high, key_low, key_high, key_low], axis=1)
    scores = lax.dot_general(
        query_cat,
        key_cat,
        (((1,), (1,)), ((), ())),
        preferred_element_type=jnp.float32,
    )
    weights = jnp.exp2(scores - jnp.max(scores, axis=1, keepdims=True))
    weight_sum = jnp.sum(weights, axis=1, keepdims=True)
    weight_high, weight_low = halves(weights)
    wide = plain_dot(weight_high, jnp.concatenate([value_high, value_low], axis=1))
    mixture = wide[:, :HEAD_G] + wide[:, HEAD_G:] + plain_dot(weight_low, value_high)
    mixture = mixture / weight_sum
    mixture = jnp.concatenate([mixture, jnp.zeros_like(mixture)], axis=1)
    result_ref[...] = mixture.reshape(HEADS_G, tokens, 2 * HEAD_G)

    head_id, my_part = me // copies, me // HEADS_G

    def third(index):
        peer = line[index][0]
        return pltpu.make_async_remote_copy(
            src_ref=result_ref.at[peer % HEADS_G],
            dst_ref=attended_ref.at[head_id],
            send_sem=send_three.at[index],
            recv_sem=recv_three.at[index],
            device_id=(blk, peer),
            device_id_type=MESH,
        )

    for index, (peer, source) in enumerate(line):

        @pl.when(peer // HEADS_G == part)
        def _(index=index):
            third(index).start()

    @pl.when(my_part == part)
    def _():
        attended_ref[head_id] = result_ref[me % HEADS_G]

    for fetch in fetches[1:]:
        fetch.wait()
    for index, (peer, source) in enumerate(line):

        @pl.when(source % copies == my_part)
        def _(index=index):
            third(index).wait_recv()

    attended = jnp.concatenate([attended_ref[h, :, :HEAD_G] for h in range(HEADS_G)], axis=1)
    mixed = two_ref[...] + split_dot(attended, output_ref[...])
    up = one_ref[...] + split_dot(mixed, split_second_ref[...])
    mid = up.shape[1] // 4
    up = jnp.concatenate([up[:, g * mid : (g + 1) * mid] for g in range(4)], axis=0)
    fine = split_dot(up, split_first_ref[...])
    cells_down, cells_across = rows // 4, cols // 4
    chunks = spread_ref.shape[0]
    for a in range(2):
        for b in range(2):
            for i in range(cells_down):
                top = ((2 * a + b) * cells_down + i) * cells_across
                for c in range(2):
                    for d in range(2):
                        at = (4 * i + 2 * a + c) * cols + 2 * b + d
                        for chunk in range(chunks):
                            lane = ((2 * c + d) * chunks + chunk) * LANES
                            spread_ref[chunk, pl.ds(at, cells_across, stride=4)] = fine[
                                top : top + cells_across, lane : lane + LANES
                            ]
    for chunk in range(chunks):
        lanes = slice(chunk * LANES, (chunk + 1) * LANES)
        refined_ref[:, lanes] = zero_ref[:, lanes] + spread_ref[chunk]

    for copy in first + second:
        copy.wait_send()
    for index, (peer, source) in enumerate(line):

        @pl.when(peer // HEADS_G == part)
        def _(index=index):
            third(index).wait_send()


def global_part(grid, normed, two, one, zero, scale, project, output, split_second, split_first):
    sizes = (lax.axis_size("blk"), lax.axis_size("head"))
    blocks, group = sizes
    tokens, width = normed.shape
    vmem = pl.BlockSpec(memory_space=pltpu.VMEM)
    hbm = pl.BlockSpec(memory_space=pl.ANY)
    f32, dma = jnp.float32, pltpu.SemaphoreType.DMA
    held = (blocks + 1) * tokens

    def body(*refs):
        global_kernel(sizes, *refs, grid)

    return pl.pallas_call(
        body,
        out_shape=jax.ShapeDtypeStruct(zero.shape, f32),
        in_specs=[vmem] * 4 + [pl.BlockSpec(memory_space=pltpu.SMEM)] + [hbm] * 4,
        out_specs=vmem,
        scratch_shapes=[
            pltpu.VMEM((blocks, tokens, width), f32),
            pltpu.VMEM((blocks, tokens, project.shape[1]), f32),
            pltpu.VMEM((HEADS_G, held, 2 * HEAD_G), f32),
            pltpu.VMEM((group, held, 2 * HEAD_G), f32),
            pltpu.VMEM((HEADS_G, tokens, 2 * HEAD_G), f32),
            pltpu.VMEM((HEADS_G, tokens, 2 * HEAD_G), f32),
            pltpu.VMEM((zero.shape[1] // LANES, zero.shape[0], LANES), f32),
            pltpu.VMEM(project.shape, f32),
            pltpu.VMEM(output.shape, f32),
            pltpu.VMEM(split_second.shape, f32),
            pltpu.VMEM(split_first.shape, f32),
            dma((4,)),
            dma((blocks - 1,)),
            dma((blocks - 1,)),
            dma((group - 1,)),
            dma((group - 1,)),
            dma((group - 1,)),
            dma((group - 1,)),
        ],
        compiler_params=pltpu.CompilerParams(
            collective_id=1, has_side_effects=True, vmem_limit_bytes=48 * 2**20
        ),
        name="global_part",
    )(normed, two, one, zero, scale[None], project, output, split_second, split_first)


def shards(
    latent,
    local_gain,
    local_project,
    local_output,
    local_scale,
    merge_first,
    merge_second,
    global_gain,
    global_project,
    global_output,
    global_scale,
    split_second,
    split_first,
):
    tile_rows, tile_cols = (latent.shape[0], latent.shape[1])
    level_zero, level_one, level_two, normed_two = local_part(
        latent,
        local_gain,
        local_project,
        local_output,
        local_scale,
        merge_first,
        merge_second,
        global_gain,
    )
    refined = global_part(
        (tile_rows, tile_cols),
        normed_two,
        level_two,
        level_one,
        level_zero,
        global_scale,
        global_project,
        global_output,
        split_second,
        split_first,
    )
    return refined.reshape(tile_rows, tile_cols, C0)


def solution(mesh):
    in_specs = (P("blk", "head", None), P(), P(), P(), P(), P(), P(), P(), P(), P(), P(), P(), P())
    out_specs = P("blk", "head", None)
    return jax.shard_map(shards, mesh=mesh, in_specs=in_specs, out_specs=out_specs, check_vma=False)
```

```python
import math

import jax
import jax.numpy as jnp
from jax import lax
from jax.experimental import pallas as pl
from jax.experimental.pallas import tpu as pltpu
from jax.sharding import PartitionSpec as P

C0 = 256
HEAD0 = 64
HEADS_G = 8
HEAD_G = 64


EPSILON = 1e-06
FLOOR_VALUE = 0.5


def rms_scale(values, gains):
    return values * lax.rsqrt(jnp.mean(values * values, axis=-1, keepdims=True) + EPSILON) * gains


def floor_rows(values):
    return values * lax.rsqrt(
        jnp.maximum(jnp.mean(values * values, axis=-1, keepdims=True), FLOOR_VALUE)
    )


MESH = pl.DeviceIdType.MESH
HALO = 3
EDGE = 8
LANES = 128
LOG2E = math.log2(math.e)
DIRECTIONS = ((-1, 0), (1, 0), (0, -1), (0, 1), (-1, -1), (-1, 1), (1, -1), (1, 1))


def halves(values):
    high = values.astype(jnp.bfloat16)
    return high, (values - high.astype(jnp.float32)).astype(jnp.bfloat16)


def plain_dot(left, right):
    return jnp.dot(left, right, preferred_element_type=jnp.float32)


def weight_dot(values, pair):
    weight_high, weight_low = pair[0][...], pair[1][...]
    high, low = halves(values)
    count = values.shape[0]
    if count > 128:
        return (
            plain_dot(low, weight_high)
            + plain_dot(high, weight_low)
            + plain_dot(high, weight_high)
        )
    both = plain_dot(jnp.concatenate([high, low], axis=0), weight_high)
    return both[count:] + plain_dot(high, weight_low) + both[:count]


def group_matrix(width, group):
    rows = lax.broadcasted_iota(jnp.int32, (width, width), 0) // group
    cols = lax.broadcasted_iota(jnp.int32, (width, width), 1) // group
    return jnp.where(rows == cols, 1.0 / group, 0.0).astype(jnp.bfloat16)


def group_mean_squares(values, group):
    high, low = halves(values * values)
    matrix = group_matrix(values.shape[1], group)
    return plain_dot(high, matrix) + plain_dot(low, matrix)


def neighbours(sizes):
    blk, head = lax.axis_index("blk"), lax.axis_index("head")
    for dz, dc in DIRECTIONS:
        row, col = blk + dz, head + dc
        back_row, back_col = blk - dz, head - dc
        there = (row >= 0) & (row < sizes[0]) & (col >= 0) & (col < sizes[1])
        back = (back_row >= 0) & (back_row < sizes[0]) & (back_col >= 0) & (back_col < sizes[1])
        yield (row, col), there, back


def local_kernel(
    sizes,
    latent_hbm,
    latent_ref,
    gain_ref,
    scale_ref,
    global_gain_ref,
    prepare,
    fetch_small,
    pairs,
    one_ref,
    two_ref,
    normed_ref,
    up_ref,
    down_ref,
    left_ref,
    right_ref,
    query_ref,
    key_ref,
    high_ref,
    low_ref,
    attended_ref,
    zero_chunks,
    one_chunks,
    send_sem,
    recv_sem,
):
    rows, cols, width = latent_ref.shape
    heads = width // HEAD0
    span = cols + EDGE
    low_row, low_col = rows - HALO, cols - EDGE
    blk, head = lax.axis_index("blk"), lax.axis_index("head")
    sources = {-1: slice(0, HALO), 1: slice(low_row, rows)}
    corner_rows = {-1: slice(rows + HALO, rows + 2 * HALO), 1: slice(0, HALO)}
    columns = {-1: slice(0, EDGE), 1: slice(low_col, cols)}

    def copy_of(index, device):
        dz, dc = DIRECTIONS[index]
        if dc == 0:
            source = latent_hbm.at[sources[dz]]
            target = down_ref if dz < 0 else up_ref
        else:
            side = right_ref if dc < 0 else left_ref
            if dz == 0:
                source = latent_hbm.at[:, columns[dc]]
                target = side.at[HALO : HALO + rows]
            else:
                source = latent_hbm.at[sources[dz], columns[dc]]
                target = side.at[corner_rows[dz]]
        return pltpu.make_async_remote_copy(
            src_ref=source,
            dst_ref=target,
            send_sem=send_sem.at[index],
            recv_sem=recv_sem.at[index],
            device_id=device,
            device_id_type=MESH,
        )

    for index, (device, there, back) in enumerate(neighbours(sizes)):

        @pl.when(there)
        def _(index=index, device=device):
            copy_of(index, device).start()

    fetch_small()
    prepare(0)
    gain = gain_ref[...]
    head_factor = jnp.concatenate(
        [jnp.broadcast_to(scale_ref[:, h : h + 1], (1, HEAD0)) for h in range(heads)],
        axis=1,
    )
    head_factor = head_factor * (LOG2E / HEAD0)
    latent = latent_ref[...].reshape(rows * cols, width)
    normed = rms_scale(latent, gain)
    queries = weight_dot(normed, [ref.at[:, :width] for ref in pairs[0]])
    queries = queries * lax.rsqrt(group_mean_squares(queries, HEAD0) + EPSILON) * head_factor
    high, low = halves(queries)
    for h in range(heads):
        a, b = high[:, h * HEAD0 : (h + 1) * HEAD0], low[:, h * HEAD0 : (h + 1) * HEAD0]
        query_ref[h] = jnp.concatenate([a, a, b, b], axis=1)
    for index in (1, 2, 3):
        prepare(index)

    for index, (device, there, back) in enumerate(neighbours(sizes)):

        @pl.when(back)
        def _(index=index, device=device):
            copy_of(index, device).wait_recv()

        @pl.when(there)
        def _(index=index, device=device):
            copy_of(index, device).wait_send()

    has_up, has_down = blk > 0, blk < sizes[0] - 1
    has_left, has_right = head > 0, head < sizes[1] - 1
    middle = jnp.concatenate(
        [
            jnp.where(has_up, up_ref[...], 0.0),
            latent_ref[...],
            jnp.where(has_down, down_ref[...], 0.0),
        ],
        axis=0,
    )
    shape = (rows + 2 * HALO, EDGE, width)
    spot = lax.broadcasted_iota(jnp.int32, shape, 1)
    layer = lax.broadcasted_iota(jnp.int32, shape, 0)
    row_there = (has_up | (layer >= HALO)) & (has_down | (layer < rows + HALO))
    side = jnp.where(
        (spot < HALO) & has_right & row_there,
        right_ref[...],
        jnp.where((spot >= EDGE - HALO) & has_left & row_there, left_ref[...], 0.0),
    )
    padded_rows = rows + 2 * HALO
    total = padded_rows * span
    everything = jnp.concatenate([middle, side], axis=1).reshape(total, width)
    keyvals = weight_dot(
        rms_scale(everything, gain), [ref.at[:, width:] for ref in pairs[0]]
    )
    keys = keyvals[:, :width]
    keys = keys * lax.rsqrt(group_mean_squares(keys, HEAD0) + EPSILON)
    high, low = halves(keys)
    value_high, value_low = halves(keyvals[:, width:])
    for h in range(heads):
        part = slice(h * HEAD0, (h + 1) * HEAD0)
        a, b = high[:, part], low[:, part]
        key_ref[h] = jnp.concatenate([a, b, a, b], axis=1)
        high_ref[h] = jnp.concatenate([value_high[:, part], value_low[:, part]], axis=1)
        low_ref[h] = value_high[:, part]

    step_rows = 4
    block = step_rows * cols
    reach = (step_rows + 2 * HALO) * span
    query_at = lax.broadcasted_iota(jnp.int32, (block, 1), 0)
    key_at = lax.broadcasted_iota(jnp.int32, (1, reach), 1)
    query_row, query_col = query_at // cols, query_at % cols
    key_row, place = key_at // span, key_at % span
    key_col = jnp.where(
        place < cols + HALO,
        place,
        jnp.where(place >= span - HALO, place - span, -4 * span),
    )
    col_here = (
        (key_col + head * cols >= 0)
        & (key_col + head * cols < sizes[1] * cols)
    )
    key_col = jnp.where(col_here, key_col, -4 * span)
    row_gap, col_gap = key_row - query_row, key_col - query_col
    near = (row_gap >= 0) & (row_gap <= 2 * HALO) & (col_gap >= -HALO) & (col_gap <= HALO)
    near_bias = jnp.where(near, 0.0, -1e30)

    def attend(step, unused):
        grid_row = blk * rows + step * step_rows - HALO + key_row
        bias = near_bias + jnp.where(
            (grid_row >= 0) & (grid_row < sizes[0] * rows), 0.0, -1e30
        )
        queries_at = pl.ds(pl.multiple_of(step * block, block), block)
        keys_at = pl.ds(pl.multiple_of(step * step_rows * span, step_rows * span), reach)
        parts = []
        for h in range(heads):
            scores = (
                lax.dot_general(
                    query_ref[h, queries_at],
                    key_ref[h, keys_at],
                    (((1,), (1,)), ((), ())),
                    preferred_element_type=jnp.float32,
                )
                + bias
            )
            weights = jnp.exp2(scores - jnp.max(scores, axis=1, keepdims=True))
            weight_sum = jnp.sum(weights, axis=1, keepdims=True)
            weight_high, weight_low = halves(weights)
            wide = plain_dot(weight_high, high_ref[h, keys_at])
            mixture = (
                wide[:, :HEAD0]
                + wide[:, HEAD0:]
                + plain_dot(weight_low, low_ref[h, keys_at])
            )
            parts.append(mixture / weight_sum)
        attended_ref[queries_at] = jnp.concatenate(parts, axis=1)
        return unused

    lax.fori_loop(0, rows // step_rows, attend, 0)
    zero = latent + weight_dot(attended_ref[...], pairs[1])
    store_chunks(zero_chunks, zero)
    merged = merge_from(zero_chunks, rows, cols)
    one = weight_dot(merged, pairs[2])
    store_chunks(one_chunks, one)
    merged = merge_from(one_chunks, rows // 2, cols // 2)
    one_ref[...] = merged
    two = weight_dot(merged, pairs[3])
    two_ref[...] = two
    normed_ref[...] = rms_scale(two, global_gain_ref[...])


def store_chunks(ref, values):
    for chunk in range(ref.shape[0]):
        ref[chunk] = values[:, chunk * LANES : (chunk + 1) * LANES]


def merge_from(ref, rows, cols):
    cells, width = rows * cols, ref.shape[0] * LANES
    evens, odds = (
        jnp.concatenate(
            [
                ref[chunk, pl.ds(start, cells // 2, stride=2)]
                for chunk in range(ref.shape[0])
            ],
            axis=1,
        ).reshape(rows // 2, 2, cols // 2, width)
        for start in (0, 1)
    )
    pieces = [
        source[:, which].reshape(cells // 4, width)
        for which in (0, 1)
        for source in (evens, odds)
    ]
    return jnp.concatenate(pieces, axis=1)


def global_kernel(
    sizes,
    grid,
    scale_ref,
    prepare,
    pairs,
    one_ref,
    two_ref,
    normed_ref,
    zero_chunks,
    refined_ref,
    gather_ref,
    outgoing_ref,
    incoming_ref,
    result_ref,
    attended_ref,
    spread_ref,
    send_one,
    recv_one,
    send_two,
    recv_two,
    send_three,
    recv_three,
):
    blocks, group = sizes
    rows, cols = grid
    tokens, width = normed_ref.shape
    copies = group // HEADS_G
    blk, me = lax.axis_index("blk"), lax.axis_index("head")
    column = [((blk + d) % blocks, (blk + blocks - d) % blocks) for d in range(1, blocks)]
    line = [((me + d) % group, (me + group - d) % group) for d in range(1, group)]

    first = [
        pltpu.make_async_remote_copy(
            src_ref=normed_ref,
            dst_ref=gather_ref.at[index],
            send_sem=send_one.at[index],
            recv_sem=recv_one.at[index],
            device_id=(peer, me),
            device_id_type=MESH,
        )
        for index, (peer, unused) in enumerate(column)
    ]
    for copy in first:
        copy.start()
    prepare(4)
    own_rows = 2 * tokens
    stages = (slice(0, own_rows), slice(own_rows, own_rows + (blocks - 1) * tokens))

    def second(stage, index):
        peer = line[index][0]
        return pltpu.make_async_remote_copy(
            src_ref=outgoing_ref.at[peer // copies, stages[stage]],
            dst_ref=incoming_ref.at[me, stages[stage]],
            send_sem=send_two.at[stage, index],
            recv_sem=recv_two.at[stage, index],
            device_id=(blk, peer),
            device_id_type=MESH,
        )

    def key_values(projected, h):
        start = 3 * HEAD_G * h
        keys = floor_rows(projected[:, start + HEAD_G : start + 2 * HEAD_G])
        values = projected[:, start + 2 * HEAD_G : start + 3 * HEAD_G]
        return jnp.concatenate([keys, values], axis=1)

    own = weight_dot(normed_ref[...], pairs[4])
    blank = jnp.zeros((tokens, HEAD_G), jnp.float32)
    for h in range(HEADS_G):
        start = 3 * HEAD_G * h
        queries = floor_rows(own[:, start : start + HEAD_G])
        outgoing_ref[h, :tokens] = key_values(own, h)
        outgoing_ref[h, tokens:own_rows] = jnp.concatenate([queries, blank], axis=1)
    for index in range(group - 1):
        second(0, index).start()
    for index in (5, 6, 7):
        prepare(index)
    for copy in first:
        copy.wait_recv()
    gathered = gather_ref[...].reshape((blocks - 1) * tokens, width)
    projected = weight_dot(gathered, pairs[4])
    for h in range(HEADS_G):
        outgoing_ref[h, own_rows:] = key_values(projected, h)
    for index in range(group - 1):
        second(1, index).start()
    incoming_ref[me] = outgoing_ref[me // copies]
    for index in range(group - 1):
        for stage in range(2):
            second(stage, index).wait_recv()

    lane_of = lax.broadcasted_iota(jnp.int32, scale_ref.shape, 1)
    own_scale = jnp.where(lane_of == me // copies, scale_ref[...], 0.0)
    factor = jnp.sum(own_scale, axis=1, keepdims=True) * (LOG2E / HEAD_G)
    part = me % copies
    queries = incoming_ref[pl.ds(part * HEADS_G, HEADS_G), tokens:own_rows, :HEAD_G]
    high, low = halves(queries.reshape(HEADS_G * tokens, HEAD_G) * factor)
    query_cat = jnp.concatenate([high, high, low, low], axis=1)
    keyvals = jnp.concatenate([incoming_ref[:, :tokens], incoming_ref[:, own_rows:]], axis=1)
    keyvals = keyvals.reshape(group * blocks * tokens, 2 * HEAD_G)
    high, low = halves(keyvals)
    key_high, key_low = high[:, :HEAD_G], low[:, :HEAD_G]
    value_high, value_low = high[:, HEAD_G:], low[:, HEAD_G:]
    key_cat = jnp.concatenate([key_high, key_low, key_high, key_low], axis=1)
    scores = lax.dot_general(
        query_cat,
        key_cat,
        (((1,), (1,)), ((), ())),
        preferred_element_type=jnp.float32,
    )
    weights = jnp.exp2(scores - jnp.max(scores, axis=1, keepdims=True))
    weight_sum = jnp.sum(weights, axis=1, keepdims=True)
    weight_high, weight_low = halves(weights)
    wide = plain_dot(weight_high, jnp.concatenate([value_high, value_low], axis=1))
    mixture = wide[:, :HEAD_G] + wide[:, HEAD_G:] + plain_dot(weight_low, value_high)
    mixture = mixture / weight_sum
    mixture = jnp.concatenate([mixture, jnp.zeros_like(mixture)], axis=1)
    result_ref[...] = mixture.reshape(HEADS_G, tokens, 2 * HEAD_G)

    head_id, my_part = me // copies, me // HEADS_G

    def third(index):
        peer = line[index][0]
        return pltpu.make_async_remote_copy(
            src_ref=result_ref.at[peer % HEADS_G],
            dst_ref=attended_ref.at[head_id],
            send_sem=send_three.at[index],
            recv_sem=recv_three.at[index],
            device_id=(blk, peer),
            device_id_type=MESH,
        )

    for index, (peer, source) in enumerate(line):

        @pl.when(peer // HEADS_G == part)
        def _(index=index):
            third(index).start()

    @pl.when(my_part == part)
    def _():
        attended_ref[head_id] = result_ref[me % HEADS_G]

    for index, (peer, source) in enumerate(line):

        @pl.when(source % copies == my_part)
        def _(index=index):
            third(index).wait_recv()

    attended = jnp.concatenate([attended_ref[h, :, :HEAD_G] for h in range(HEADS_G)], axis=1)
    mixed = two_ref[...] + weight_dot(attended, pairs[5])
    up = one_ref[...] + weight_dot(mixed, pairs[6])
    mid = up.shape[1] // 4
    up = jnp.concatenate([up[:, g * mid : (g + 1) * mid] for g in range(4)], axis=0)
    fine = weight_dot(up, pairs[7])
    cells_down, cells_across = rows // 4, cols // 4
    chunks = spread_ref.shape[0]
    for a in range(2):
        for b in range(2):
            for i in range(cells_down):
                top = ((2 * a + b) * cells_down + i) * cells_across
                for c in range(2):
                    for d in range(2):
                        at = (4 * i + 2 * a + c) * cols + 2 * b + d
                        for chunk in range(chunks):
                            lane = ((2 * c + d) * chunks + chunk) * LANES
                            spread_ref[chunk, pl.ds(at, cells_across, stride=4)] = fine[
                                top : top + cells_across, lane : lane + LANES
                            ]
    for chunk in range(chunks):
        lanes = slice(chunk * LANES, (chunk + 1) * LANES)
        refined_ref[:, lanes] = zero_chunks[chunk] + spread_ref[chunk]

    for copy in first:
        copy.wait_send()
    for index in range(group - 1):
        for stage in range(2):
            second(stage, index).wait_send()
    for index, (peer, source) in enumerate(line):

        @pl.when(peer // HEADS_G == part)
        def _(index=index):
            third(index).wait_send()


SMALL = (1, 4, 7, 10)
LARGE = (2, 3, 5, 6, 8, 9, 11, 12)


def whole_kernel(sizes, inputs, output, staged, highs, lows, kept, local_scratch, global_scratch, sems):
    input_sem, send_sem, recv_sem, *global_sems = sems
    rows, cols = inputs[0].shape[:2]
    barrier = pltpu.get_barrier_semaphore()
    blk, head = lax.axis_index("blk"), lax.axis_index("head")

    fetches = [
        pltpu.make_async_copy(source, target, input_sem.at[index])
        for index, (source, target) in enumerate(zip(inputs, staged))
    ]
    count = jnp.int32(sizes[0] + sizes[1] - 2)
    for d in range(1, sizes[0]):
        peer = (blk + d) % sizes[0]
        pl.semaphore_signal(barrier, inc=1, device_id=(peer, head), device_id_type=MESH)
    for d in range(1, sizes[1]):
        peer = (head + d) % sizes[1]
        pl.semaphore_signal(barrier, inc=1, device_id=(blk, peer), device_id_type=MESH)
    for (dz, dc), (device, there, back) in zip(DIRECTIONS, neighbours(sizes)):
        if dz and dc:
            count = count + there.astype(jnp.int32)

            @pl.when(there)
            def _(device=device):
                pl.semaphore_signal(barrier, inc=1, device_id=device, device_id_type=MESH)

    for fetch in fetches:
        fetch.start()
    pl.semaphore_wait(barrier, count)

    def prepare(which):
        index = LARGE[which]
        fetches[index].wait()
        highs[which][...], lows[which][...] = halves(staged[index][...])

    def fetch_small():
        for index in (0,) + SMALL:
            fetches[index].wait()

    pairs = list(zip(highs, lows))
    one_ref, two_ref, normed_ref = kept
    local_kernel(
        sizes,
        inputs[0],
        staged[0],
        staged[1],
        staged[4],
        staged[7],
        prepare,
        fetch_small,
        pairs,
        one_ref,
        two_ref,
        normed_ref,
        *local_scratch,
        send_sem,
        recv_sem,
    )
    global_kernel(
        sizes,
        (rows, cols),
        staged[10],
        prepare,
        pairs,
        one_ref,
        two_ref,
        normed_ref,
        local_scratch[-2],
        output,
        *global_scratch,
        *global_sems,
    )


def shards(*arrays):
    arrays = [array[None] if array.ndim == 1 else array for array in arrays]
    rows, cols, width = arrays[0].shape
    sizes = (lax.axis_size("blk"), lax.axis_size("head"))
    blocks, group = sizes
    heads = width // HEAD0
    total = (rows + 2 * HALO) * (cols + EDGE)
    mid, coarse = arrays[5].shape[1], arrays[6].shape[1]
    tokens = rows * cols // 16
    held = (blocks + 1) * tokens
    f32, b16, dma = jnp.float32, jnp.bfloat16, pltpu.SemaphoreType.DMA
    weights = [pltpu.VMEM(arrays[index].shape, b16) for index in LARGE]
    scratch = (
        [pltpu.VMEM(array.shape, f32) for array in arrays],
        weights,
        weights,
        [
            pltpu.VMEM((tokens, 4 * mid), f32),
            pltpu.VMEM((tokens, coarse), f32),
            pltpu.VMEM((tokens, coarse), f32),
        ],
        [
            pltpu.VMEM((HALO, cols, width), f32),
            pltpu.VMEM((HALO, cols, width), f32),
            pltpu.VMEM((rows + 2 * HALO, EDGE, width), f32),
            pltpu.VMEM((rows + 2 * HALO, EDGE, width), f32),
            pltpu.VMEM((heads, rows * cols, 4 * HEAD0), b16),
            pltpu.VMEM((heads, total, 4 * HEAD0), b16),
            pltpu.VMEM((heads, total, 2 * HEAD0), b16),
            pltpu.VMEM((heads, total, HEAD0), b16),
            pltpu.VMEM((rows * cols, width), f32),
            pltpu.VMEM((width // LANES, rows * cols, LANES), f32),
            pltpu.VMEM((mid // LANES, rows * cols // 4, LANES), f32),
        ],
        [
            pltpu.VMEM((blocks - 1, tokens, coarse), f32),
            pltpu.VMEM((HEADS_G, held, 2 * HEAD_G), f32),
            pltpu.VMEM((group, held, 2 * HEAD_G), f32),
            pltpu.VMEM((HEADS_G, tokens, 2 * HEAD_G), f32),
            pltpu.VMEM((HEADS_G, tokens, 2 * HEAD_G), f32),
            pltpu.VMEM((width // LANES, rows * cols, LANES), f32),
        ],
        [
            dma((len(arrays),)),
            dma((8,)),
            dma((8,)),
            dma((blocks - 1,)),
            dma((blocks - 1,)),
            dma((2, group - 1)),
            dma((2, group - 1)),
            dma((group - 1,)),
            dma((group - 1,)),
        ],
    )

    def body(*refs):
        refs = list(refs)
        inputs, output, rest = refs[: len(arrays)], refs[len(arrays)], refs[len(arrays) + 1 :]
        parts = []
        for shapes in scratch:
            parts.append(rest[: len(shapes)])
            rest = rest[len(shapes) :]
        whole_kernel(sizes, inputs, output, *parts)

    refined = pl.pallas_call(
        body,
        out_shape=jax.ShapeDtypeStruct((rows * cols, width), f32),
        in_specs=[pl.BlockSpec(memory_space=pl.ANY)] * len(arrays),
        out_specs=pl.BlockSpec(memory_space=pltpu.VMEM),
        scratch_shapes=[shape for shapes in scratch for shape in shapes],
        compiler_params=pltpu.CompilerParams(
            collective_id=0, has_side_effects=True, vmem_limit_bytes=60 * 2**20
        ),
        name="window",
    )(*arrays)
    return refined.reshape(rows, cols, width)


def solution(mesh):
    in_specs = (P("blk", "head", None), P(), P(), P(), P(), P(), P(), P(), P(), P(), P(), P(), P())
    out_specs = P("blk", "head", None)
    return jax.shard_map(shards, mesh=mesh, in_specs=in_specs, out_specs=out_specs, check_vma=False)
```

```python
import math

import jax
import jax.numpy as jnp
from jax import lax
from jax.experimental import pallas as pl
from jax.experimental.pallas import tpu as pltpu
from jax.sharding import PartitionSpec as P

C0 = 256
HEAD0 = 64
HEADS_G = 8
HEAD_G = 64


EPSILON = 1e-06
FLOOR_VALUE = 0.5


def rms_scale(values, gains):
    return values * lax.rsqrt(jnp.mean(values * values, axis=-1, keepdims=True) + EPSILON) * gains


def floor_rows(values):
    return values * lax.rsqrt(
        jnp.maximum(jnp.mean(values * values, axis=-1, keepdims=True), FLOOR_VALUE)
    )


MESH = pl.DeviceIdType.MESH
HALO = 3
EDGE = 8
LANES = 128
LOG2E = math.log2(math.e)
DIRECTIONS = ((-1, 0), (1, 0), (0, -1), (0, 1), (-1, -1), (-1, 1), (1, -1), (1, 1))


def halves(values):
    high = values.astype(jnp.bfloat16)
    return high, (values - high.astype(jnp.float32)).astype(jnp.bfloat16)


def plain_dot(left, right):
    return jnp.dot(left, right, preferred_element_type=jnp.float32)


def weight_dot(values, pair):
    weight_high, weight_low = pair[0][...], pair[1][...]
    high, low = halves(values)
    count = values.shape[0]
    if count > 128:
        return (
            plain_dot(low, weight_high)
            + plain_dot(high, weight_low)
            + plain_dot(high, weight_high)
        )
    both = plain_dot(jnp.concatenate([high, low], axis=0), weight_high)
    return both[count:] + plain_dot(high, weight_low) + both[:count]


def group_matrix(width, group):
    rows = lax.broadcasted_iota(jnp.int32, (width, width), 0) // group
    cols = lax.broadcasted_iota(jnp.int32, (width, width), 1) // group
    return jnp.where(rows == cols, 1.0 / group, 0.0).astype(jnp.bfloat16)


def group_mean_squares(values, group):
    high, low = halves(values * values)
    matrix = group_matrix(values.shape[1], group)
    return plain_dot(high, matrix) + plain_dot(low, matrix)


def neighbours(sizes):
    blk, head = lax.axis_index("blk"), lax.axis_index("head")
    for dz, dc in DIRECTIONS:
        row, col = blk + dz, head + dc
        back_row, back_col = blk - dz, head - dc
        there = (row >= 0) & (row < sizes[0]) & (col >= 0) & (col < sizes[1])
        back = (back_row >= 0) & (back_row < sizes[0]) & (back_col >= 0) & (back_col < sizes[1])
        yield (row, col), there, back


def local_kernel(
    sizes,
    latent_hbm,
    latent_ref,
    gain_ref,
    scale_ref,
    global_gain_ref,
    prepare,
    fetch_small,
    pairs,
    one_ref,
    two_ref,
    normed_ref,
    up_ref,
    down_ref,
    left_ref,
    right_ref,
    query_ref,
    key_ref,
    high_ref,
    low_ref,
    attended_ref,
    zero_chunks,
    one_chunks,
    send_sem,
    recv_sem,
):
    rows, cols, width = latent_ref.shape
    heads = width // HEAD0
    span = cols + EDGE
    low_row, low_col = rows - HALO, cols - EDGE
    blk, head = lax.axis_index("blk"), lax.axis_index("head")
    sources = {-1: slice(0, HALO), 1: slice(low_row, rows)}
    corner_rows = {-1: slice(rows + HALO, rows + 2 * HALO), 1: slice(0, HALO)}
    columns = {-1: slice(0, EDGE), 1: slice(low_col, cols)}

    def copy_of(index, device):
        dz, dc = DIRECTIONS[index]
        if dc == 0:
            source = latent_hbm.at[sources[dz]]
            target = down_ref if dz < 0 else up_ref
        else:
            side = right_ref if dc < 0 else left_ref
            if dz == 0:
                source = latent_hbm.at[:, columns[dc]]
                target = side.at[HALO : HALO + rows]
            else:
                source = latent_hbm.at[sources[dz], columns[dc]]
                target = side.at[corner_rows[dz]]
        return pltpu.make_async_remote_copy(
            src_ref=source,
            dst_ref=target,
            send_sem=send_sem.at[index],
            recv_sem=recv_sem.at[index],
            device_id=device,
            device_id_type=MESH,
        )

    for index, (device, there, back) in enumerate(neighbours(sizes)):

        @pl.when(there)
        def _(index=index, device=device):
            copy_of(index, device).start()

    fetch_small()
    prepare(0)
    gain = gain_ref[...]
    head_factor = jnp.concatenate(
        [jnp.broadcast_to(scale_ref[:, h : h + 1], (1, HEAD0)) for h in range(heads)],
        axis=1,
    )
    head_factor = head_factor * (LOG2E / HEAD0)
    latent = latent_ref[...].reshape(rows * cols, width)
    normed = rms_scale(latent, gain)
    queries = weight_dot(normed, [ref.at[:, :width] for ref in pairs[0]])
    queries = queries * lax.rsqrt(group_mean_squares(queries, HEAD0) + EPSILON) * head_factor
    high, low = halves(queries)
    for h in range(heads):
        a, b = high[:, h * HEAD0 : (h + 1) * HEAD0], low[:, h * HEAD0 : (h + 1) * HEAD0]
        query_ref[h] = jnp.concatenate([a, a, b, b], axis=1)
    for index in (1, 2, 3):
        prepare(index)

    for index, (device, there, back) in enumerate(neighbours(sizes)):

        @pl.when(back)
        def _(index=index, device=device):
            copy_of(index, device).wait_recv()

        @pl.when(there)
        def _(index=index, device=device):
            copy_of(index, device).wait_send()

    has_up, has_down = blk > 0, blk < sizes[0] - 1
    has_left, has_right = head > 0, head < sizes[1] - 1
    middle = jnp.concatenate(
        [
            jnp.where(has_up, up_ref[...], 0.0),
            latent_ref[...],
            jnp.where(has_down, down_ref[...], 0.0),
        ],
        axis=0,
    )
    shape = (rows + 2 * HALO, EDGE, width)
    spot = lax.broadcasted_iota(jnp.int32, shape, 1)
    layer = lax.broadcasted_iota(jnp.int32, shape, 0)
    row_there = (has_up | (layer >= HALO)) & (has_down | (layer < rows + HALO))
    side = jnp.where(
        (spot < HALO) & has_right & row_there,
        right_ref[...],
        jnp.where((spot >= EDGE - HALO) & has_left & row_there, left_ref[...], 0.0),
    )
    padded_rows = rows + 2 * HALO
    total = padded_rows * span
    everything = jnp.concatenate([middle, side], axis=1).reshape(total, width)
    keyvals = weight_dot(
        rms_scale(everything, gain), [ref.at[:, width:] for ref in pairs[0]]
    )
    keys = keyvals[:, :width]
    keys = keys * lax.rsqrt(group_mean_squares(keys, HEAD0) + EPSILON)
    high, low = halves(keys)
    value_high, value_low = halves(keyvals[:, width:])
    for h in range(heads):
        part = slice(h * HEAD0, (h + 1) * HEAD0)
        a, b = high[:, part], low[:, part]
        key_ref[h] = jnp.concatenate([a, b, a, b], axis=1)
        high_ref[h] = jnp.concatenate([value_high[:, part], value_low[:, part]], axis=1)
        low_ref[h] = value_high[:, part]

    step_rows = 4
    block = step_rows * cols
    reach = (step_rows + 2 * HALO) * span
    query_at = lax.broadcasted_iota(jnp.int32, (block, 1), 0)
    key_at = lax.broadcasted_iota(jnp.int32, (1, reach), 1)
    query_row, query_col = query_at // cols, query_at % cols
    key_row, place = key_at // span, key_at % span
    key_col = jnp.where(
        place < cols + HALO,
        place,
        jnp.where(place >= span - HALO, place - span, -4 * span),
    )
    col_here = (
        (key_col + head * cols >= 0)
        & (key_col + head * cols < sizes[1] * cols)
    )
    key_col = jnp.where(col_here, key_col, -4 * span)
    row_gap, col_gap = key_row - query_row, key_col - query_col
    near = (row_gap >= 0) & (row_gap <= 2 * HALO) & (col_gap >= -HALO) & (col_gap <= HALO)
    near_bias = jnp.where(near, 0.0, -1e30)

    def attend(step, unused):
        grid_row = blk * rows + step * step_rows - HALO + key_row
        bias = near_bias + jnp.where(
            (grid_row >= 0) & (grid_row < sizes[0] * rows), 0.0, -1e30
        )
        queries_at = pl.ds(pl.multiple_of(step * block, block), block)
        keys_at = pl.ds(pl.multiple_of(step * step_rows * span, step_rows * span), reach)
        parts = []
        for h in range(heads):
            scores = (
                lax.dot_general(
                    query_ref[h, queries_at],
                    key_ref[h, keys_at],
                    (((1,), (1,)), ((), ())),
                    preferred_element_type=jnp.float32,
                )
                + bias
            )
            weights = jnp.exp2(scores - jnp.max(scores, axis=1, keepdims=True))
            weight_sum = jnp.sum(weights, axis=1, keepdims=True)
            weight_high, weight_low = halves(weights)
            wide = plain_dot(weight_high, high_ref[h, keys_at])
            mixture = (
                wide[:, :HEAD0]
                + wide[:, HEAD0:]
                + plain_dot(weight_low, low_ref[h, keys_at])
            )
            parts.append(mixture / weight_sum)
        attended_ref[queries_at] = jnp.concatenate(parts, axis=1)
        return unused

    lax.fori_loop(0, rows // step_rows, attend, 0)
    zero = latent + weight_dot(attended_ref[...], pairs[1])
    store_chunks(zero_chunks, zero)
    merged = merge_from(zero_chunks, rows, cols)
    one = weight_dot(merged, pairs[2])
    store_chunks(one_chunks, one)
    merged = merge_from(one_chunks, rows // 2, cols // 2)
    one_ref[...] = merged
    two = weight_dot(merged, pairs[3])
    two_ref[...] = two
    normed_ref[...] = rms_scale(two, global_gain_ref[...])


def store_chunks(ref, values):
    for chunk in range(ref.shape[0]):
        ref[chunk] = values[:, chunk * LANES : (chunk + 1) * LANES]


def merge_from(ref, rows, cols):
    cells, width = rows * cols, ref.shape[0] * LANES
    evens, odds = (
        jnp.concatenate(
            [
                ref[chunk, pl.ds(start, cells // 2, stride=2)]
                for chunk in range(ref.shape[0])
            ],
            axis=1,
        ).reshape(rows // 2, 2, cols // 2, width)
        for start in (0, 1)
    )
    pieces = [
        source[:, which].reshape(cells // 4, width)
        for which in (0, 1)
        for source in (evens, odds)
    ]
    return jnp.concatenate(pieces, axis=1)


def global_kernel(
    sizes,
    grid,
    scale_ref,
    prepare,
    pairs,
    one_ref,
    two_ref,
    normed_ref,
    zero_chunks,
    refined_ref,
    gather_ref,
    outgoing_ref,
    incoming_ref,
    result_ref,
    attended_ref,
    spread_ref,
    send_one,
    recv_one,
    send_two,
    recv_two,
    send_three,
    recv_three,
):
    blocks, group = sizes
    rows, cols = grid
    tokens, width = normed_ref.shape
    copies = group // HEADS_G
    blk, me = lax.axis_index("blk"), lax.axis_index("head")
    column = [((blk + d) % blocks, (blk + blocks - d) % blocks) for d in range(1, blocks)]
    line = [((me + d) % group, (me + group - d) % group) for d in range(1, group)]

    first = [
        pltpu.make_async_remote_copy(
            src_ref=normed_ref,
            dst_ref=gather_ref.at[index],
            send_sem=send_one.at[index],
            recv_sem=recv_one.at[index],
            device_id=(peer, me),
            device_id_type=MESH,
        )
        for index, (peer, unused) in enumerate(column)
    ]
    for copy in first:
        copy.start()
    prepare(4)
    own_rows = 2 * tokens
    stages = (slice(0, own_rows), slice(own_rows, own_rows + (blocks - 1) * tokens))

    def second(stage, index):
        peer = line[index][0]
        return pltpu.make_async_remote_copy(
            src_ref=outgoing_ref.at[peer // copies, stages[stage]],
            dst_ref=incoming_ref.at[me, stages[stage]],
            send_sem=send_two.at[stage, index],
            recv_sem=recv_two.at[stage, index],
            device_id=(blk, peer),
            device_id_type=MESH,
        )

    def key_values(projected, h):
        start = 3 * HEAD_G * h
        keys = floor_rows(projected[:, start + HEAD_G : start + 2 * HEAD_G])
        values = projected[:, start + 2 * HEAD_G : start + 3 * HEAD_G]
        return jnp.concatenate([keys, values], axis=1)

    own = weight_dot(normed_ref[...], pairs[4])
    blank = jnp.zeros((tokens, HEAD_G), jnp.float32)
    for h in range(HEADS_G):
        start = 3 * HEAD_G * h
        queries = floor_rows(own[:, start : start + HEAD_G])
        outgoing_ref[h, :tokens] = key_values(own, h)
        outgoing_ref[h, tokens:own_rows] = jnp.concatenate([queries, blank], axis=1)
    for index in range(group - 1):
        second(0, index).start()
    for copy in first:
        copy.wait_recv()
    gathered = gather_ref[...].reshape((blocks - 1) * tokens, width)
    projected = weight_dot(gathered, pairs[4])
    for h in range(HEADS_G):
        outgoing_ref[h, own_rows:] = key_values(projected, h)
    for index in range(group - 1):
        second(1, index).start()
    incoming_ref[me] = outgoing_ref[me // copies]
    for index in (5, 6, 7):
        prepare(index)
    for index in range(group - 1):
        for stage in range(2):
            second(stage, index).wait_recv()

    lane_of = lax.broadcasted_iota(jnp.int32, scale_ref.shape, 1)
    own_scale = jnp.where(lane_of == me // copies, scale_ref[...], 0.0)
    factor = jnp.sum(own_scale, axis=1, keepdims=True) * (LOG2E / HEAD_G)
    part = me % copies
    queries = incoming_ref[pl.ds(part * HEADS_G, HEADS_G), tokens:own_rows, :HEAD_G]
    high, low = halves(queries.reshape(HEADS_G * tokens, HEAD_G) * factor)
    query_cat = jnp.concatenate([high, high, low, low], axis=1)
    keyvals = jnp.concatenate([incoming_ref[:, :tokens], incoming_ref[:, own_rows:]], axis=1)
    keyvals = keyvals.reshape(group * blocks * tokens, 2 * HEAD_G)
    high, low = halves(keyvals)
    key_high, key_low = high[:, :HEAD_G], low[:, :HEAD_G]
    value_high, value_low = high[:, HEAD_G:], low[:, HEAD_G:]
    key_cat = jnp.concatenate([key_high, key_low, key_high, key_low], axis=1)
    scores = lax.dot_general(
        query_cat,
        key_cat,
        (((1,), (1,)), ((), ())),
        preferred_element_type=jnp.float32,
    )
    weights = jnp.exp2(scores - jnp.max(scores, axis=1, keepdims=True))
    weight_sum = jnp.sum(weights, axis=1, keepdims=True)
    weight_high, weight_low = halves(weights)
    wide = plain_dot(weight_high, jnp.concatenate([value_high, value_low], axis=1))
    mixture = wide[:, :HEAD_G] + wide[:, HEAD_G:] + plain_dot(weight_low, value_high)
    mixture = mixture / weight_sum
    mixture = jnp.concatenate([mixture, jnp.zeros_like(mixture)], axis=1)
    result_ref[...] = mixture.reshape(HEADS_G, tokens, 2 * HEAD_G)

    head_id, my_part = me // copies, me // HEADS_G

    def third(index):
        peer = line[index][0]
        return pltpu.make_async_remote_copy(
            src_ref=result_ref.at[peer % HEADS_G],
            dst_ref=attended_ref.at[head_id],
            send_sem=send_three.at[index],
            recv_sem=recv_three.at[index],
            device_id=(blk, peer),
            device_id_type=MESH,
        )

    for index, (peer, source) in enumerate(line):

        @pl.when(peer // HEADS_G == part)
        def _(index=index):
            third(index).start()

    @pl.when(my_part == part)
    def _():
        attended_ref[head_id] = result_ref[me % HEADS_G]

    for index, (peer, source) in enumerate(line):

        @pl.when(source % copies == my_part)
        def _(index=index):
            third(index).wait_recv()

    attended = jnp.concatenate([attended_ref[h, :, :HEAD_G] for h in range(HEADS_G)], axis=1)
    mixed = two_ref[...] + weight_dot(attended, pairs[5])
    up = one_ref[...] + weight_dot(mixed, pairs[6])
    mid = up.shape[1] // 4
    up = jnp.concatenate([up[:, g * mid : (g + 1) * mid] for g in range(4)], axis=0)
    fine = weight_dot(up, pairs[7])
    cells_down, cells_across = rows // 4, cols // 4
    chunks = spread_ref.shape[0]
    for a in range(2):
        for b in range(2):
            for i in range(cells_down):
                top = ((2 * a + b) * cells_down + i) * cells_across
                for c in range(2):
                    for d in range(2):
                        at = (4 * i + 2 * a + c) * cols + 2 * b + d
                        for chunk in range(chunks):
                            lane = ((2 * c + d) * chunks + chunk) * LANES
                            spread_ref[chunk, pl.ds(at, cells_across, stride=4)] = fine[
                                top : top + cells_across, lane : lane + LANES
                            ]
    for chunk in range(chunks):
        lanes = slice(chunk * LANES, (chunk + 1) * LANES)
        refined_ref[:, lanes] = zero_chunks[chunk] + spread_ref[chunk]

    for copy in first:
        copy.wait_send()
    for index in range(group - 1):
        for stage in range(2):
            second(stage, index).wait_send()
    for index, (peer, source) in enumerate(line):

        @pl.when(peer // HEADS_G == part)
        def _(index=index):
            third(index).wait_send()


SMALL = (1, 4, 7, 10)
LARGE = (2, 3, 5, 6, 8, 9, 11, 12)


def whole_kernel(sizes, inputs, output, staged, highs, lows, kept, local_scratch, global_scratch, sems):
    input_sem, send_sem, recv_sem, *global_sems = sems
    rows, cols = inputs[0].shape[:2]
    barrier = pltpu.get_barrier_semaphore()
    blk, head = lax.axis_index("blk"), lax.axis_index("head")

    fetches = [
        pltpu.make_async_copy(source, target, input_sem.at[index])
        for index, (source, target) in enumerate(zip(inputs, staged))
    ]
    count = jnp.int32(sizes[0] + sizes[1] - 2)
    for d in range(1, sizes[0]):
        peer = (blk + d) % sizes[0]
        pl.semaphore_signal(barrier, inc=1, device_id=(peer, head), device_id_type=MESH)
    for d in range(1, sizes[1]):
        peer = (head + d) % sizes[1]
        pl.semaphore_signal(barrier, inc=1, device_id=(blk, peer), device_id_type=MESH)
    for (dz, dc), (device, there, back) in zip(DIRECTIONS, neighbours(sizes)):
        if dz and dc:
            count = count + there.astype(jnp.int32)

            @pl.when(there)
            def _(device=device):
                pl.semaphore_signal(barrier, inc=1, device_id=device, device_id_type=MESH)

    for fetch in fetches:
        fetch.start()
    pl.semaphore_wait(barrier, count)

    def prepare(which):
        index = LARGE[which]
        fetches[index].wait()
        highs[which][...], lows[which][...] = halves(staged[index][...])

    def fetch_small():
        for index in (0,) + SMALL:
            fetches[index].wait()

    pairs = list(zip(highs, lows))
    one_ref, two_ref, normed_ref = kept
    local_kernel(
        sizes,
        inputs[0],
        staged[0],
        staged[1],
        staged[4],
        staged[7],
        prepare,
        fetch_small,
        pairs,
        one_ref,
        two_ref,
        normed_ref,
        *local_scratch,
        send_sem,
        recv_sem,
    )
    global_kernel(
        sizes,
        (rows, cols),
        staged[10],
        prepare,
        pairs,
        one_ref,
        two_ref,
        normed_ref,
        local_scratch[-2],
        output,
        *global_scratch,
        *global_sems,
    )


def shards(*arrays):
    arrays = [array[None] if array.ndim == 1 else array for array in arrays]
    rows, cols, width = arrays[0].shape
    sizes = (lax.axis_size("blk"), lax.axis_size("head"))
    blocks, group = sizes
    heads = width // HEAD0
    total = (rows + 2 * HALO) * (cols + EDGE)
    mid, coarse = arrays[5].shape[1], arrays[6].shape[1]
    tokens = rows * cols // 16
    held = (blocks + 1) * tokens
    f32, b16, dma = jnp.float32, jnp.bfloat16, pltpu.SemaphoreType.DMA
    weights = [pltpu.VMEM(arrays[index].shape, b16) for index in LARGE]
    scratch = (
        [pltpu.VMEM(array.shape, f32) for array in arrays],
        weights,
        weights,
        [
            pltpu.VMEM((tokens, 4 * mid), f32),
            pltpu.VMEM((tokens, coarse), f32),
            pltpu.VMEM((tokens, coarse), f32),
        ],
        [
            pltpu.VMEM((HALO, cols, width), f32),
            pltpu.VMEM((HALO, cols, width), f32),
            pltpu.VMEM((rows + 2 * HALO, EDGE, width), f32),
            pltpu.VMEM((rows + 2 * HALO, EDGE, width), f32),
            pltpu.VMEM((heads, rows * cols, 4 * HEAD0), b16),
            pltpu.VMEM((heads, total, 4 * HEAD0), b16),
            pltpu.VMEM((heads, total, 2 * HEAD0), b16),
            pltpu.VMEM((heads, total, HEAD0), b16),
            pltpu.VMEM((rows * cols, width), f32),
            pltpu.VMEM((width // LANES, rows * cols, LANES), f32),
            pltpu.VMEM((mid // LANES, rows * cols // 4, LANES), f32),
        ],
        [
            pltpu.VMEM((blocks - 1, tokens, coarse), f32),
            pltpu.VMEM((HEADS_G, held, 2 * HEAD_G), f32),
            pltpu.VMEM((group, held, 2 * HEAD_G), f32),
            pltpu.VMEM((HEADS_G, tokens, 2 * HEAD_G), f32),
            pltpu.VMEM((HEADS_G, tokens, 2 * HEAD_G), f32),
            pltpu.VMEM((width // LANES, rows * cols, LANES), f32),
        ],
        [
            dma((len(arrays),)),
            dma((8,)),
            dma((8,)),
            dma((blocks - 1,)),
            dma((blocks - 1,)),
            dma((2, group - 1)),
            dma((2, group - 1)),
            dma((group - 1,)),
            dma((group - 1,)),
        ],
    )

    def body(*refs):
        refs = list(refs)
        inputs, output, rest = refs[: len(arrays)], refs[len(arrays)], refs[len(arrays) + 1 :]
        parts = []
        for shapes in scratch:
            parts.append(rest[: len(shapes)])
            rest = rest[len(shapes) :]
        whole_kernel(sizes, inputs, output, *parts)

    refined = pl.pallas_call(
        body,
        out_shape=jax.ShapeDtypeStruct((rows * cols, width), f32),
        in_specs=[pl.BlockSpec(memory_space=pl.ANY)] * len(arrays),
        out_specs=pl.BlockSpec(memory_space=pltpu.VMEM),
        scratch_shapes=[shape for shapes in scratch for shape in shapes],
        compiler_params=pltpu.CompilerParams(
            collective_id=0, has_side_effects=True, vmem_limit_bytes=60 * 2**20
        ),
        name="window",
    )(*arrays)
    return refined.reshape(rows, cols, width)


def solution(mesh):
    in_specs = (P("blk", "head", None), P(), P(), P(), P(), P(), P(), P(), P(), P(), P(), P(), P())
    out_specs = P("blk", "head", None)
    return jax.shard_map(shards, mesh=mesh, in_specs=in_specs, out_specs=out_specs, check_vma=False)
```
